512 devices in a mesh: brow: 16 (over y, z_lo), bcol: 32 (over x, z_hi, core).
Axes of the slice: x: 4, y: 8, z: 8 (z_hi: 4, z_lo: 2; z = z_hi * 2 + z_lo), core: 2. Of those that a mesh axis runs over, the one named last changes fastest.
Arguments:
- scores: float32 [32, 1024, 128], P('bcol', 'brow'), may hold values from 0.01 to 32
- degree: int32 [32, 1024], P('bcol', 'brow'), may hold values from 50 to 200
- seed_mask: int32 [32, 1024], P('bcol', 'brow'), may hold values 0 or 1
- tiles: bfloat16 [16, 32, 64, 128, 128], P('brow', 'bcol'), may hold values from 0 to 2, as said below
- tile_list: int32 [16, 32, 2, 64], P('brow', 'bcol'), may hold values from 0 to 15, as said below
- tile_count: int32 [16, 32], P('brow', 'bcol'), may hold values from 1 to 64, as said below
Outputs:
- propagated: float32 [32, 1024, 128], P('bcol', 'brow')
The draws below stay inside these ranges and needn't reach their ends.
Inputs may be any that keep to these rules, and one draw needn't show every extreme that they name: Slots 0 to tile_count - 1 of a device are live, the others empty; some device holds 64 live tiles. `tile_list`: entry 0 is below 16, entry 1 below 8; the live slots of a device name distinct tile blocks (a, b) with b >= a; every block (a, a) is named by a live slot. `tiles`: entries are nonnegative; a tile with a == b is symmetric and has a nonzero entry in every row; empty slots hold finite values.
All inputs are finite; a program needn't handle non-finite values. No bound on the sum of `seed_mask` on one device may be relied on, other than what follows from the above.
Results may differ from the reference program's by a relative error of at most 0.0007.
Values may be sent and summed in bfloat16 or wider, within the bound.
No kernel may reach another device: no remote copies, remote signals or barrier semaphores. Data moves between devices by JAX's collectives and lax.ppermute only.
A program may use at most 64 MiB of HBM per device.

```python
import math
import jax
import jax.numpy as jnp
from jax import lax

CLASSES = 128
TILE = 128
SWEEPS = 2
COL_ROWS = 1024
COL_TILES = 8
ROW_TILES = 16
TILE_CAP = 64
N_BROW = 16
N_BCOL = 32


def tile_layout(key):
    base = jax.random.fold_in(key, 11)
    key_order = jax.random.fold_in(base, 1)
    key_load = jax.random.fold_in(base, 2)
    key_full = jax.random.fold_in(base, 3)
    places = ROW_TILES * COL_TILES
    row_dev = jnp.arange(N_BROW, dtype=jnp.int32)[:, None, None, None]
    col_dev = jnp.arange(N_BCOL, dtype=jnp.int32)[None, :, None, None]
    local_row = jnp.arange(ROW_TILES, dtype=jnp.int32)[None, None, :, None]
    local_col = jnp.arange(COL_TILES, dtype=jnp.int32)[None, None, None, :]
    upper = col_dev + N_BCOL * local_col >= row_dev + N_BROW * local_row
    upper = jnp.broadcast_to(upper, (N_BROW, N_BCOL, ROW_TILES, COL_TILES)).reshape(N_BROW, N_BCOL, places)
    on_diag = col_dev + N_BCOL * local_col == row_dev + N_BROW * local_row
    on_diag = jnp.broadcast_to(on_diag, (N_BROW, N_BCOL, ROW_TILES, COL_TILES)).reshape(N_BROW, N_BCOL, places)
    position = jnp.arange(places, dtype=jnp.int32)
    noise = jax.random.randint(key_order, (N_BROW, N_BCOL, places), 0, 1 << 16, dtype=jnp.int32)
    ranked = jnp.where(on_diag, (1 << 16) * places + position, jnp.where(upper, noise * places + position, -1 - position))
    _, chosen = lax.top_k(ranked, TILE_CAP)
    chosen = chosen.astype(jnp.int32)
    entries = jnp.stack([chosen // COL_TILES, chosen % COL_TILES], axis=2).astype(jnp.int32)
    avail = jnp.sum(upper.astype(jnp.int32), axis=-1)
    drawn = TILE_CAP // (1 + jax.random.randint(key_load, (N_BROW, N_BCOL), 0, 4, dtype=jnp.int32))
    count = jnp.minimum(drawn, avail)
    diag_dev = jnp.arange(N_BCOL, dtype=jnp.int32)[None, :] % N_BROW == jnp.arange(N_BROW, dtype=jnp.int32)[:, None]
    count = jnp.where(diag_dev, jnp.maximum(count, COL_TILES), count)
    full_col = jax.random.randint(key_full, (), 0, N_BCOL, dtype=jnp.int32)
    target = (jnp.arange(N_BROW, dtype=jnp.int32)[:, None] == 0) & (jnp.arange(N_BCOL, dtype=jnp.int32)[None, :] == full_col)
    count = jnp.where(target, TILE_CAP, count).astype(jnp.int32)
    return (entries, count)


def draw_tile_list(key, part):
    return tile_layout(key)[0]


def draw_tile_count(key, part):
    return tile_layout(key)[1]


def draw_tiles(key, part):
    entries, count = tile_layout(key)
    value_key = jax.random.fold_in(key, 29)
    keep_key = jax.random.fold_in(key, 31)
    pair_key = jax.random.fold_in(key, 37)
    shape = (N_BROW, N_BCOL, TILE_CAP, TILE, TILE)
    values = jnp.exp(jax.random.uniform(value_key, shape, jnp.float32, math.log(0.1), math.log(2.0)))
    keep = jax.random.randint(keep_key, shape, 0, TILE, dtype=jnp.int32) == 0
    ranks = jax.random.randint(pair_key, shape[:-1], 0, 1 << 16, dtype=jnp.int32) * TILE + jnp.arange(TILE, dtype=jnp.int32)
    partner = jnp.argsort(ranks, axis=-1).astype(jnp.int32)
    paired = partner[..., None] == jnp.arange(TILE, dtype=jnp.int32)
    row_dev = jnp.arange(N_BROW, dtype=jnp.int32)[:, None, None]
    col_dev = jnp.arange(N_BCOL, dtype=jnp.int32)[None, :, None]
    same = row_dev + N_BROW * entries[:, :, 0] == col_dev + N_BCOL * entries[:, :, 1]
    same_tile = same[..., None, None]
    linked_diag = keep | jnp.swapaxes(keep, -1, -2) | paired | jnp.swapaxes(paired, -1, -2)
    linked = jnp.where(same_tile, linked_diag, keep)
    mirrored = 0.5 * (values + jnp.swapaxes(values, -1, -2))
    chosen = jnp.where(same_tile, mirrored, values)
    return jnp.where(linked, chosen, 0.0).astype(jnp.bfloat16)


def draw_scores(key, part):
    base_key = jax.random.fold_in(key, 41)
    class_key = jax.random.fold_in(key, 43)
    shape = (N_BCOL, COL_ROWS, CLASSES)
    base = jnp.exp(jax.random.uniform(base_key, shape, jnp.float32, math.log(0.01), math.log(4.0)))
    leading = jax.random.randint(class_key, (N_BCOL, COL_TILES), 0, CLASSES, dtype=jnp.int32)
    per_row = jnp.repeat(leading, TILE, axis=1)
    marked = per_row[:, :, None] == jnp.arange(CLASSES, dtype=jnp.int32)[None, None, :]
    return jnp.where(marked, 8.0 * base, base).astype(jnp.float32)


def touch_ends(values, rng, least, largest):
    longest = values.shape.index(max(values.shape))
    spots = []
    for shift in (0, 1):
        where = [jax.random.randint(jax.random.fold_in(rng, axis), (), 0, length) for axis, length in enumerate(values.shape)]
        where[longest] = (where[longest] + shift) % values.shape[longest]
        spots.append(tuple(where))
    return values.at[spots[0]].set(least).at[spots[1]].set(largest)


def setup_inputs(seed: int = 0) -> dict:
    seeds = jax.random.split(jax.random.key(seed), 7)
    return {
        "scores": draw_scores(jax.random.fold_in(seeds[6], 71), 0),
        "degree": touch_ends(jax.random.randint(seeds[1], (N_BCOL, COL_ROWS), 50, 201), jax.random.fold_in(seeds[1], 1), 50, 200).astype(jnp.int32),
        "seed_mask": touch_ends((jax.random.randint(seeds[2], (N_BCOL, COL_ROWS), 0, 8) < 1).astype(jnp.int32), jax.random.fold_in(seeds[2], 1), 0, 1),
        "tiles": draw_tiles(jax.random.fold_in(seeds[6], 71), 0),
        "tile_list": draw_tile_list(jax.random.fold_in(seeds[6], 71), 0),
        "tile_count": draw_tile_count(jax.random.fold_in(seeds[6], 71), 0),
    }


def row_weights(field):
    total = jnp.sum(field, axis=-1, keepdims=True)
    share = field / total
    entropy = -jnp.sum(share * jnp.log(share), axis=-1, keepdims=True)
    return (2.0 - entropy / math.log(field.shape[-1])) * field


def reference(scores, degree, seed_mask, tiles, tile_list, tile_count):
    ratio = N_BCOL // N_BROW
    scale = degree.astype(jnp.float32)[:, :, None]
    seeded = seed_mask[:, :, None] > 0
    slot_ids = jnp.arange(TILE_CAP, dtype=jnp.int32)

    def sweep_once(field):
        message = row_weights(field).reshape(N_BCOL, COL_TILES, TILE, CLASSES)

        def per_device(carry, index):
            row_dev = index // N_BCOL
            col_dev = index % N_BCOL
            stored = tiles[row_dev, col_dev].astype(jnp.float32)
            local_row = tile_list[row_dev, col_dev, 0]
            local_col = tile_list[row_dev, col_dev, 1]
            live = slot_ids < tile_count[row_dev, col_dev]
            a_col = row_dev + N_BROW * (local_row % ratio)
            a_tile = local_row // ratio
            same = (row_dev + N_BROW * local_row) == (col_dev + N_BCOL * local_col)
            col_pick = message[col_dev][local_col].astype(jnp.float32)
            row_pick = message[a_col, a_tile].astype(jnp.float32)
            forward = jnp.einsum("sij,sjk->sik", stored, col_pick, precision=lax.Precision.HIGHEST)
            forward = forward * live.astype(jnp.float32)[:, None, None]
            mirror = jnp.einsum("sji,sjk->sik", stored, row_pick, precision=lax.Precision.HIGHEST)
            mirror = mirror * (live & jnp.logical_not(same)).astype(jnp.float32)[:, None, None]
            carry = carry.at[a_col, a_tile].add(forward)
            carry = carry.at[col_dev, local_col].add(mirror)
            return carry, None

        start = jnp.zeros((N_BCOL, COL_TILES, TILE, CLASSES), jnp.float32)
        total, _ = lax.scan(per_device, start, jnp.arange(N_BROW * N_BCOL, dtype=jnp.int32))
        total = total.reshape(N_BCOL, COL_ROWS, CLASSES)
        return jnp.where(seeded, scores, total / scale)

    field = scores
    for sweep in range(SWEEPS):
        field = sweep_once(field)
    return field
```

```python
import math

import jax
import jax.numpy as jnp
from jax import lax
from jax.experimental import pallas as pl
from jax.experimental.pallas import tpu as pltpu
from jax.sharding import PartitionSpec as P

SWEEPS = 2
HEAD = 16
STEPS = 3840.0
SCALE_STEPS = 64.0
TINY = 1e-37
VMEM = 48 * 1024 * 1024


def encode(x):
    biggest = jnp.max(jnp.max(x, axis=0, keepdims=True), axis=1, keepdims=True)
    scale = jnp.floor(jnp.log(jnp.maximum(biggest, TINY)) * SCALE_STEPS) + 2.0
    below = jnp.log(jnp.maximum(x, TINY)) - scale * (1.0 / SCALE_STEPS)
    code = jnp.clip(below * STEPS + 65535.5, 0.0, 65535.0)
    code = jnp.where(x > 0.0, code, 0.0).astype(jnp.int32) - 32768
    head = jnp.broadcast_to(scale, (HEAD, x.shape[1])).astype(jnp.int32)
    return code.astype(jnp.int16), head.astype(jnp.int16)


def decode(piece):
    rows = piece.shape[0] - HEAD
    code = piece[:rows].astype(jnp.int32).astype(jnp.float32)
    head = piece[rows:].astype(jnp.int32).astype(jnp.float32)[:1]
    base = head * (1.0 / SCALE_STEPS) - 32767.0 / STEPS
    return jnp.where(code > -32768.0, jnp.exp(code * (1.0 / STEPS) + base), 0.0)


def weighted(field):
    total = jnp.maximum(jnp.sum(field, axis=-1, keepdims=True), TINY)
    share = field / total
    entropy = -jnp.sum(share * jnp.log(jnp.maximum(share, TINY)), axis=-1, keepdims=True)
    return (2.0 - entropy / math.log(field.shape[-1])) * field


def put_message(field, copies_ref, one_ref):
    rows = field.shape[0]
    code, head = encode(weighted(field))
    one_ref[:rows] = code
    one_ref[rows:] = head
    for i in range(copies_ref.shape[0]):
        copies_ref[i, :rows] = code
        copies_ref[i, rows:] = head


def split(value):
    high = value.astype(jnp.bfloat16)
    return high, (value - high.astype(jnp.float32)).astype(jnp.bfloat16)


def first_kernel(scores_ref, copies_ref, one_ref):
    put_message(scores_ref[...], copies_ref, one_ref)


def copies_kernel(after_ref, one_ref, copies_ref):
    for i in range(copies_ref.shape[0]):
        copies_ref[i] = one_ref[...]


def forward_kernel(meta_ref, got_ref, tiles_ref, keep_ref, send_ref, msg, acc):
    pieces = got_ref.shape[0]
    rows = got_ref.shape[1] - HEAD
    size = tiles_ref.shape[-1]
    classes = got_ref.shape[2]
    for i in range(pieces):
        high, low = split(decode(got_ref[i]))
        msg[i * rows : (i + 1) * rows, :classes] = high
        msg[i * rows : (i + 1) * rows, classes:] = low
    acc[...] = jnp.zeros_like(acc)

    def body(s, carry):
        col = meta_ref[0, s]
        row = meta_ref[1, s]
        part = jnp.dot(
            tiles_ref[s], msg[pl.ds(pl.multiple_of(col * size, size), size), :],
            preferred_element_type=jnp.float32,
        )
        where = pl.ds(pl.multiple_of(row * size, size), size)
        acc[where, :] += part[:, :classes] + part[:, classes:]
        return carry

    lax.fori_loop(0, tiles_ref.shape[0], body, 0, unroll=8)
    core = meta_ref[4, 0]
    kept = keep_ref.shape[0]
    for j in range(kept):
        p = 2 * (j % (kept // 2)) + j // (kept // 2)
        keep_ref[j] = acc[pl.ds(pl.multiple_of(p * size + core * rows, rows), rows), :]
        send_ref[j] = acc[pl.ds(pl.multiple_of(p * size + (1 - core) * rows, rows), rows), :]


def join_kernel(after_ref, keep_ref, got_ref, out_ref):
    rows = keep_ref.shape[1]
    for j in range(keep_ref.shape[0]):
        code, head = encode(keep_ref[j] + got_ref[j])
        out_ref[j, :rows] = code
        out_ref[j, rows:] = head


def mirror_kernel(meta_ref, own_ref, other_ref, tiles_ref, out_ref, msg, acc):
    pieces = own_ref.shape[0]
    rows = own_ref.shape[1] - HEAD
    size = tiles_ref.shape[-1]
    classes = own_ref.shape[2]
    core = meta_ref[4, 0]
    for j in range(pieces):
        p = 2 * (j % (pieces // 2)) + j // (pieces // 2)
        for ref, half in ((own_ref, core), (other_ref, 1 - core)):
            high, low = split(decode(ref[j]))
            where = pl.ds(pl.multiple_of(p * size + half * rows, rows), rows)
            msg[where, :classes] = high
            msg[where, classes:] = low
    acc[...] = jnp.zeros_like(acc)

    def body(s, carry):
        row = meta_ref[2, s]
        col = meta_ref[3, s]
        part = lax.dot_general(
            tiles_ref[s], msg[pl.ds(pl.multiple_of(row * size, size), size), :],
            (((0,), (0,)), ((), ())), preferred_element_type=jnp.float32,
        )
        where = pl.ds(pl.multiple_of(col * size, size), size)
        acc[where, :] += part[:, :classes] + part[:, classes:]
        return carry

    lax.fori_loop(0, tiles_ref.shape[0], body, 0, unroll=8)
    for i in range(out_ref.shape[0]):
        code, head = encode(acc[i * rows : (i + 1) * rows, :])
        out_ref[i, :rows] = code
        out_ref[i, rows:] = head


def total_of(ref):
    total = decode(ref[0])
    for i in range(1, ref.shape[0]):
        total = total + decode(ref[i])
    return total


def sum_kernel(got_ref, out_ref):
    out_ref[...] = total_of(got_ref)


def next_field(got_ref, row_ref, scores_ref, scale_ref, seed_ref):
    total = total_of(got_ref) + row_ref[...]
    return jnp.where(seed_ref[...] > 0.0, scores_ref[...], total / scale_ref[...])


def middle_kernel(got_ref, row_ref, scores_ref, scale_ref, seed_ref, copies_ref, one_ref):
    field = next_field(got_ref, row_ref, scores_ref, scale_ref, seed_ref)
    put_message(field, copies_ref, one_ref)


def last_kernel(got_ref, row_ref, scores_ref, scale_ref, seed_ref, out_ref):
    out_ref[...] = next_field(got_ref, row_ref, scores_ref, scale_ref, seed_ref)


WHOLE = pl.BlockSpec(memory_space=pltpu.VMEM)
SCALARS = pl.BlockSpec(memory_space=pltpu.SMEM)
ANYWHERE = pl.BlockSpec(memory_space=pl.ANY)


def call(kernel, name, outs, args, specs=None, scratch=()):
    single = not isinstance(outs, (tuple, list))
    return pl.pallas_call(
        kernel,
        out_shape=outs,
        in_specs=specs or [WHOLE] * len(args),
        out_specs=WHOLE if single else tuple(WHOLE for _ in outs),
        scratch_shapes=list(scratch),
        compiler_params=pltpu.CompilerParams(vmem_limit_bytes=VMEM),
        name=name,
    )(*args)


def on_device(scores, degree, seed_mask, tiles, tile_list, tile_count):
    n_brow = lax.axis_size("brow")
    n_bcol = lax.axis_size("bcol")
    ratio = n_bcol // n_brow
    rows = scores.shape[1]
    classes = scores.shape[2]
    capacity = tiles.shape[2]
    size = tiles.shape[-1]
    col_tiles = n_brow * rows // size
    row_tiles = ratio * col_tiles
    my_row = lax.axis_index("brow")
    my_col = lax.axis_index("bcol")
    stored = tiles[0, 0]
    local_row = jnp.clip(tile_list[0, 0, 0], 0, row_tiles - 1)
    local_col = jnp.clip(tile_list[0, 0, 1], 0, col_tiles - 1)
    live = jnp.arange(capacity, dtype=jnp.int32) < tile_count[0, 0]
    same = my_row + n_brow * local_row == my_col + n_bcol * local_col
    meta = jnp.stack([
        local_col,
        jnp.where(live, local_row, row_tiles),
        local_row,
        jnp.where(live & jnp.logical_not(same), local_col, col_tiles),
        jnp.full((capacity,), my_col % 2, jnp.int32),
    ])
    initial = scores[0]
    seeds = jnp.broadcast_to(seed_mask[0].astype(jnp.float32)[:, None], (rows, classes))
    scale = jnp.broadcast_to(degree[0].astype(jnp.float32)[:, None], (rows, classes))

    half = n_bcol // 2
    groups = [[2 * j + k for j in range(half)] for k in range(2)]
    exchange = [(i, i ^ 1) for i in range(n_bcol)]
    transpose = [
        (a * n_bcol + n_brow * h + b, b * n_bcol + n_brow * h + a)
        for a in range(n_brow) for h in range(ratio) for b in range(n_brow)
    ]

    def swap(value):
        return lax.ppermute(value, ("brow", "bcol"), transpose)

    def over_brow(value):
        return lax.all_to_all(value, "brow", split_axis=0, concat_axis=0, tiled=True)

    def over_bcol(value):
        return lax.all_to_all(
            value, "bcol", split_axis=0, concat_axis=0, tiled=True, axis_index_groups=groups
        )

    piece = jax.ShapeDtypeStruct((rows + HEAD, classes), jnp.int16)
    brow_pieces = jax.ShapeDtypeStruct((n_brow,) + piece.shape, jnp.int16)
    bcol_pieces = jax.ShapeDtypeStruct((half,) + piece.shape, jnp.int16)
    sums = jax.ShapeDtypeStruct((half, rows, classes), jnp.float32)
    share = jax.ShapeDtypeStruct((rows, classes), jnp.float32)

    copies, one = call(first_kernel, "first", (brow_pieces, piece), (initial,))
    for sweep in range(SWEEPS):
        col_got = over_brow(copies)
        copies = call(
            copies_kernel, "copies", bcol_pieces, (col_got, swap(one)), [ANYWHERE, WHOLE]
        )
        row_own = over_bcol(copies)
        keep, send = call(
            forward_kernel, "forward", (sums, sums), (meta, col_got, stored),
            [SCALARS, WHOLE, WHOLE],
            [pltpu.VMEM((col_tiles * size, 2 * classes), jnp.bfloat16),
             pltpu.VMEM(((row_tiles + 1) * size, classes), jnp.float32)],
        )
        got = lax.ppermute(send, "bcol", exchange)
        joined = call(
            join_kernel, "join", bcol_pieces, (row_own, keep, got), [ANYWHERE, WHOLE, WHOLE]
        )
        row_got = over_bcol(joined)
        row_other = lax.ppermute(row_own, "bcol", exchange)
        col_parts = call(
            mirror_kernel, "mirror", brow_pieces, (meta, row_own, row_other, stored),
            [SCALARS, WHOLE, WHOLE, WHOLE],
            [pltpu.VMEM((row_tiles * size, 2 * classes), jnp.bfloat16),
             pltpu.VMEM(((col_tiles + 1) * size, classes), jnp.float32)],
        )
        col_sums = over_brow(col_parts)
        row_sum = swap(call(sum_kernel, "sum", share, (row_got,)))
        args = (col_sums, row_sum, initial, scale, seeds)
        if sweep < SWEEPS - 1:
            copies, one = call(middle_kernel, "middle", (brow_pieces, piece), args)
        else:
            field = call(last_kernel, "last", share, args)
    return field[None]


def solution(mesh):
    placed = (
        P("bcol", "brow", None),
        P("bcol", "brow"),
        P("bcol", "brow"),
        P("brow", "bcol", None, None, None),
        P("brow", "bcol", None, None),
        P("brow", "bcol"),
    )
    return jax.shard_map(
        on_device, mesh=mesh, in_specs=placed, out_specs=P("bcol", "brow", None), check_vma=False
    )
```

```python
import math

import jax
import jax.numpy as jnp
from jax import lax
from jax.experimental import pallas as pl
from jax.experimental.pallas import tpu as pltpu
from jax.sharding import PartitionSpec as P

SWEEPS = 2
HEAD = 16
STEPS = 3840.0
SCALE_STEPS = 64.0
TINY = 1e-37
VMEM = 24 * 1024 * 1024


def encode(x):
    biggest = jnp.max(jnp.max(x, axis=0, keepdims=True), axis=1, keepdims=True)
    scale = jnp.floor(jnp.log(jnp.maximum(biggest, TINY)) * SCALE_STEPS) + 2.0
    below = jnp.log(jnp.maximum(x, TINY)) - scale * (1.0 / SCALE_STEPS)
    code = jnp.clip(below * STEPS + 65535.5, 0.0, 65535.0)
    code = jnp.where(x > 0.0, code, 0.0).astype(jnp.int32) - 32768
    head = jnp.broadcast_to(scale, (HEAD, x.shape[1])).astype(jnp.int32)
    return code.astype(jnp.int16), head.astype(jnp.int16)


def decode(piece):
    rows = piece.shape[0] - HEAD
    code = piece[:rows].astype(jnp.int32).astype(jnp.float32)
    head = piece[rows:].astype(jnp.int32).astype(jnp.float32)[:1]
    base = head * (1.0 / SCALE_STEPS) - 32767.0 / STEPS
    return jnp.where(code > -32768.0, jnp.exp(code * (1.0 / STEPS) + base), 0.0)


def weighted(field):
    total = jnp.maximum(jnp.sum(field, axis=-1, keepdims=True), TINY)
    share = field / total
    entropy = -jnp.sum(share * jnp.log(jnp.maximum(share, TINY)), axis=-1, keepdims=True)
    return (2.0 - entropy / math.log(field.shape[-1])) * field


def put_message(field, copies_ref, one_ref):
    rows = field.shape[0]
    code, head = encode(weighted(field))
    one_ref[:rows] = code
    one_ref[rows:] = head
    for i in range(copies_ref.shape[0]):
        copies_ref[i, :rows] = code
        copies_ref[i, rows:] = head


def split(value):
    high = value.astype(jnp.bfloat16)
    return high, (value - high.astype(jnp.float32)).astype(jnp.bfloat16)


def first_kernel(scores_ref, copies_ref, one_ref):
    put_message(scores_ref[...], copies_ref, one_ref)


def copies_kernel(after_ref, one_ref, copies_ref):
    for i in range(copies_ref.shape[0]):
        copies_ref[i] = one_ref[...]


def place(list_ref, count_ref, slot, row_tiles, col_tiles):
    n_brow, n_bcol = lax.axis_size("brow"), lax.axis_size("bcol")
    row = jnp.clip(list_ref[0, slot], 0, row_tiles - 1)
    col = jnp.clip(list_ref[1, slot], 0, col_tiles - 1)
    live = slot < count_ref[0, 0]
    same = lax.axis_index("brow") + n_brow * row == lax.axis_index("bcol") + n_bcol * col
    return row, col, live, same


def held_at(held_ref, column, rows):
    return pl.multiple_of(held_ref[lax.axis_index("brow"), column] * rows, rows)


def forward_kernel(
    list_ref, count_ref, held_ref, got_ref, tiles_ref, keep_ref, send_ref, msg, acc
):
    pieces, rows, classes = got_ref.shape[0], got_ref.shape[1] - HEAD, got_ref.shape[2]
    size = tiles_ref.shape[-1]
    col_tiles = msg.shape[0] // size
    row_tiles = acc.shape[0] // size - 1
    for i in range(pieces):
        high, low = split(decode(got_ref[i]))
        msg[i * rows : (i + 1) * rows, :classes] = high
        msg[i * rows : (i + 1) * rows, classes:] = low
    acc[...] = jnp.zeros_like(acc)

    def body(s, carry):
        row, col, live, _ = place(list_ref, count_ref, s, row_tiles, col_tiles)
        part = jnp.dot(
            tiles_ref[s], msg[pl.ds(pl.multiple_of(col * size, size), size), :],
            preferred_element_type=jnp.float32,
        )
        row = jnp.where(live, row, row_tiles)
        where = pl.ds(pl.multiple_of(row * size, size), size)
        acc[where, :] += part[:, :classes] + part[:, classes:]
        return carry

    lax.fori_loop(0, tiles_ref.shape[0], body, 0, unroll=8)
    core = lax.rem(lax.axis_index("bcol"), 2)
    for j in range(keep_ref.shape[0]):
        keep_ref[j] = acc[pl.ds(held_at(held_ref, 2 * j + core, rows), rows), :]
        send_ref[j] = acc[pl.ds(held_at(held_ref, 2 * j + 1 - core, rows), rows), :]


def join_kernel(keep_ref, got_ref, out_ref):
    rows = keep_ref.shape[1]
    for j in range(keep_ref.shape[0]):
        code, head = encode(keep_ref[j] + got_ref[j])
        out_ref[j, :rows] = code
        out_ref[j, rows:] = head


def mirror_kernel(
    list_ref, count_ref, held_ref, own_ref, other_ref, tiles_ref, out_ref, msg, acc
):
    pieces, rows, classes = own_ref.shape[0], own_ref.shape[1] - HEAD, own_ref.shape[2]
    size = tiles_ref.shape[-1]
    row_tiles = msg.shape[0] // size
    col_tiles = acc.shape[0] // size - 1
    core = lax.rem(lax.axis_index("bcol"), 2)
    for j in range(pieces):
        for ref, column in ((own_ref, 2 * j + core), (other_ref, 2 * j + 1 - core)):
            high, low = split(decode(ref[j]))
            where = pl.ds(held_at(held_ref, column, rows), rows)
            msg[where, :classes] = high
            msg[where, classes:] = low
    acc[...] = jnp.zeros_like(acc)

    def body(s, carry):
        row, col, live, same = place(list_ref, count_ref, s, row_tiles, col_tiles)
        part = lax.dot_general(
            tiles_ref[s], msg[pl.ds(pl.multiple_of(row * size, size), size), :],
            (((0,), (0,)), ((), ())), preferred_element_type=jnp.float32,
        )
        col = jnp.where(live & jnp.logical_not(same), col, col_tiles)
        where = pl.ds(pl.multiple_of(col * size, size), size)
        acc[where, :] += part[:, :classes] + part[:, classes:]
        return carry

    lax.fori_loop(0, tiles_ref.shape[0], body, 0, unroll=8)
    for i in range(out_ref.shape[0]):
        code, head = encode(acc[i * rows : (i + 1) * rows, :])
        out_ref[i, :rows] = code
        out_ref[i, rows:] = head


def total_of(ref):
    total = decode(ref[0])
    for i in range(1, ref.shape[0]):
        total = total + decode(ref[i])
    return total


def sum_kernel(got_ref, out_ref):
    out_ref[...] = total_of(got_ref)


def next_field(got_ref, row_ref, scores_ref, scale_ref, seed_ref):
    total = total_of(got_ref) + row_ref[...]
    return jnp.where(seed_ref[...] > 0.0, scores_ref[...], total / scale_ref[...])


def middle_kernel(got_ref, row_ref, scores_ref, scale_ref, seed_ref, copies_ref, one_ref):
    field = next_field(got_ref, row_ref, scores_ref, scale_ref, seed_ref)
    put_message(field, copies_ref, one_ref)


def last_kernel(got_ref, row_ref, scores_ref, scale_ref, seed_ref, out_ref):
    out_ref[...] = next_field(got_ref, row_ref, scores_ref, scale_ref, seed_ref)


def hops(a, b):
    def chip(device):
        r, c = device
        return c // 8, r // 2, c // 2 % 4 * 2 + r % 2

    steps = (abs(i - j) for i, j in zip(chip(a), chip(b)))
    return sum(min(step, length - step) for step, length in zip(steps, (4, 8, 8)))


def cheapest(cost):
    n = len(cost)
    u, v, match, way = [0] * (n + 1), [0] * (n + 1), [0] * (n + 1), [0] * (n + 1)
    for i in range(1, n + 1):
        match[0], j0 = i, 0
        least, used = [math.inf] * (n + 1), [False] * (n + 1)
        while match[j0]:
            used[j0] = True
            i0, delta, j1 = match[j0], math.inf, 0
            for j in range(1, n + 1):
                if not used[j]:
                    now = cost[i0 - 1][j - 1] - u[i0] - v[j]
                    if now < least[j]:
                        least[j], way[j] = now, j0
                    if least[j] < delta:
                        delta, j1 = least[j], j
            for j in range(n + 1):
                if used[j]:
                    u[match[j]] += delta
                    v[j] -= delta
                else:
                    least[j] -= delta
            j0 = j1
        while j0:
            match[j0] = match[way[j0]]
            j0 = way[j0]
    columns = [0] * n
    for j in range(1, n + 1):
        columns[match[j] - 1] = j - 1
    return columns


def holders(n_brow, n_bcol):
    pairs, pieces = [], []
    for r in range(n_brow):
        owners = [(b, c) for c in range(r, n_bcol, n_brow) for b in range(n_brow)]
        cost = [[hops(owner, (r, k)) ** 6 for k in range(n_bcol)] for owner in owners]
        held = [0] * n_bcol
        for (b, c), k in zip(owners, cheapest(cost)):
            pairs.append((b * n_bcol + c, r * n_bcol + k))
            held[k] = 2 * (b // 2 * (n_bcol // n_brow) + c // n_brow) + b % 2
        pieces.append(held)
    return pairs, pieces


WHOLE = pl.BlockSpec(memory_space=pltpu.VMEM)
SCALARS = pl.BlockSpec(memory_space=pltpu.SMEM)
ANYWHERE = pl.BlockSpec(memory_space=pl.ANY)


def call(kernel, name, outs, args, specs=None, scratch=()):
    single = not isinstance(outs, (tuple, list))
    return pl.pallas_call(
        kernel,
        out_shape=outs,
        in_specs=specs or [WHOLE] * len(args),
        out_specs=WHOLE if single else tuple(WHOLE for _ in outs),
        scratch_shapes=list(scratch),
        compiler_params=pltpu.CompilerParams(vmem_limit_bytes=VMEM),
        name=name,
    )(*args)


def on_device(scores, degree, seed_mask, tiles, tile_list, tile_count):
    n_brow = lax.axis_size("brow")
    n_bcol = lax.axis_size("bcol")
    ratio = n_bcol // n_brow
    rows = scores.shape[1]
    classes = scores.shape[2]
    capacity = tiles.shape[2]
    size = tiles.shape[-1]
    col_tiles = n_brow * rows // size
    row_tiles = ratio * col_tiles
    stored = tiles[0, 0]
    slots = tile_list[0, 0]
    pairs, pieces = holders(n_brow, n_bcol)
    held = jnp.asarray(pieces, jnp.int32)
    initial = scores[0]
    seeds = jnp.broadcast_to(seed_mask[0].astype(jnp.float32)[:, None], (rows, classes))
    scale = jnp.broadcast_to(degree[0].astype(jnp.float32)[:, None], (rows, classes))

    half = n_bcol // 2
    groups = [[2 * j + k for j in range(half)] for k in range(2)]
    exchange = [(i, i ^ 1) for i in range(n_bcol)]
    back = [(holder, owner) for owner, holder in pairs]

    def swap(value, way):
        return lax.ppermute(value, ("brow", "bcol"), way)

    def over_brow(value):
        return lax.all_to_all(value, "brow", split_axis=0, concat_axis=0, tiled=True)

    def over_bcol(value):
        return lax.all_to_all(
            value, "bcol", split_axis=0, concat_axis=0, tiled=True, axis_index_groups=groups
        )

    piece = jax.ShapeDtypeStruct((rows + HEAD, classes), jnp.int16)
    brow_pieces = jax.ShapeDtypeStruct((n_brow,) + piece.shape, jnp.int16)
    bcol_pieces = jax.ShapeDtypeStruct((half,) + piece.shape, jnp.int16)
    sums = jax.ShapeDtypeStruct((half, rows, classes), jnp.float32)
    share = jax.ShapeDtypeStruct((rows, classes), jnp.float32)

    copies, one = call(first_kernel, "first", (brow_pieces, piece), (initial,))
    for sweep in range(SWEEPS):
        col_got = over_brow(copies)
        copies = call(
            copies_kernel, "copies", bcol_pieces, (col_got, swap(one, pairs)), [ANYWHERE, WHOLE]
        )
        row_own = over_bcol(copies)
        keep, send = call(
            forward_kernel, "forward", (sums, sums), (slots, tile_count, held, col_got, stored),
            [SCALARS, SCALARS, SCALARS, WHOLE, WHOLE],
            [pltpu.VMEM((col_tiles * size, 2 * classes), jnp.bfloat16),
             pltpu.VMEM(((row_tiles + 1) * size, classes), jnp.float32)],
        )
        got = lax.ppermute(send, "bcol", exchange)
        joined = call(join_kernel, "join", bcol_pieces, (keep, got))
        row_got = over_bcol(joined)
        row_other = lax.ppermute(row_own, "bcol", exchange)
        col_parts = call(
            mirror_kernel, "mirror", brow_pieces,
            (slots, tile_count, held, row_own, row_other, stored),
            [SCALARS, SCALARS, SCALARS, WHOLE, WHOLE, WHOLE],
            [pltpu.VMEM((row_tiles * size, 2 * classes), jnp.bfloat16),
             pltpu.VMEM(((col_tiles + 1) * size, classes), jnp.float32)],
        )
        col_sums = over_brow(col_parts)
        row_sum = swap(call(sum_kernel, "sum", share, (row_got,)), back)
        args = (col_sums, row_sum, initial, scale, seeds)
        if sweep < SWEEPS - 1:
            copies, one = call(middle_kernel, "middle", (brow_pieces, piece), args)
        else:
            field = call(last_kernel, "last", share, args)
    return field[None]


def solution(mesh):
    placed = (
        P("bcol", "brow", None),
        P("bcol", "brow"),
        P("bcol", "brow"),
        P("brow", "bcol", None, None, None),
        P("brow", "bcol", None, None),
        P("brow", "bcol"),
    )
    return jax.shard_map(
        on_device, mesh=mesh, in_specs=placed, out_specs=P("bcol", "brow", None), check_vma=False
    )
```

```python
import math

import jax
import jax.numpy as jnp
from jax import lax
from jax.experimental import pallas as pl
from jax.experimental.pallas import tpu as pltpu
from jax.sharding import PartitionSpec as P

SWEEPS = 2
HEAD = 16
STEPS = 3840.0
SCALE_STEPS = 64.0
TINY = 1e-37
VMEM = 24 * 1024 * 1024


def encode(x):
    biggest = jnp.max(jnp.max(x, axis=0, keepdims=True), axis=1, keepdims=True)
    scale = jnp.floor(jnp.log(jnp.maximum(biggest, TINY)) * SCALE_STEPS) + 2.0
    below = jnp.log(jnp.maximum(x, TINY)) - scale * (1.0 / SCALE_STEPS)
    code = jnp.clip(below * STEPS + 65535.5, 0.0, 65535.0)
    code = jnp.where(x > 0.0, code, 0.0).astype(jnp.int32) - 32768
    head = jnp.broadcast_to(scale, (HEAD, x.shape[1])).astype(jnp.int32)
    return code.astype(jnp.int16), head.astype(jnp.int16)


def decode(piece):
    rows = piece.shape[0] - HEAD
    code = piece[:rows].astype(jnp.int32).astype(jnp.float32)
    head = piece[rows:].astype(jnp.int32).astype(jnp.float32)[:1]
    base = head * (1.0 / SCALE_STEPS) - 32767.0 / STEPS
    return jnp.where(code > -32768.0, jnp.exp(code * (1.0 / STEPS) + base), 0.0)


def weighted(field):
    total = jnp.maximum(jnp.sum(field, axis=-1, keepdims=True), TINY)
    share = field / total
    entropy = -jnp.sum(share * jnp.log(jnp.maximum(share, TINY)), axis=-1, keepdims=True)
    return (2.0 - entropy / math.log(field.shape[-1])) * field


def put_message(field, copies_ref, one_ref):
    rows = field.shape[0]
    code, head = encode(weighted(field))
    one_ref[:rows] = code
    one_ref[rows:] = head
    for i in range(copies_ref.shape[0]):
        copies_ref[i, :rows] = code
        copies_ref[i, rows:] = head


def split(value):
    high = value.astype(jnp.bfloat16)
    return high, (value - high.astype(jnp.float32)).astype(jnp.bfloat16)


def first_kernel(scores_ref, copies_ref, one_ref):
    put_message(scores_ref[...], copies_ref, one_ref)


def copies_kernel(after_ref, one_ref, copies_ref):
    for i in range(copies_ref.shape[0]):
        copies_ref[i] = one_ref[...]


def place(list_ref, count_ref, slot, row_tiles, col_tiles):
    n_brow, n_bcol = lax.axis_size("brow"), lax.axis_size("bcol")
    row = jnp.clip(list_ref[0, slot], 0, row_tiles - 1)
    col = jnp.clip(list_ref[1, slot], 0, col_tiles - 1)
    live = slot < count_ref[0, 0]
    same = lax.axis_index("brow") + n_brow * row == lax.axis_index("bcol") + n_bcol * col
    return row, col, live, same


def held_at(held_ref, column, rows):
    return pl.multiple_of(held_ref[lax.axis_index("brow"), column] * rows, rows)


def forward_kernel(
    list_ref, count_ref, held_ref, got_ref, tiles_ref, keep_ref, send_ref, msg, acc
):
    pieces, rows, classes = got_ref.shape[0], got_ref.shape[1] - HEAD, got_ref.shape[2]
    size = tiles_ref.shape[-1]
    col_tiles = msg.shape[0] // size
    row_tiles = acc.shape[0] // size - 1
    for i in range(pieces):
        high, low = split(decode(got_ref[i]))
        msg[i * rows : (i + 1) * rows, :classes] = high
        msg[i * rows : (i + 1) * rows, classes:] = low
    acc[...] = jnp.zeros_like(acc)

    def body(s, carry):
        row, col, live, _ = place(list_ref, count_ref, s, row_tiles, col_tiles)
        part = jnp.dot(
            tiles_ref[s], msg[pl.ds(pl.multiple_of(col * size, size), size), :],
            preferred_element_type=jnp.float32,
        )
        row = jnp.where(live, row, row_tiles)
        where = pl.ds(pl.multiple_of(row * size, size), size)
        acc[where, :] += part[:, :classes] + part[:, classes:]
        return carry

    lax.fori_loop(0, tiles_ref.shape[0], body, 0, unroll=16)
    core = lax.rem(lax.axis_index("bcol"), 2)
    for j in range(keep_ref.shape[0]):
        keep_ref[j] = acc[pl.ds(held_at(held_ref, 2 * j + core, rows), rows), :]
        send_ref[j] = acc[pl.ds(held_at(held_ref, 2 * j + 1 - core, rows), rows), :]


def join_kernel(keep_ref, got_ref, out_ref):
    rows = keep_ref.shape[1]
    for j in range(keep_ref.shape[0]):
        code, head = encode(keep_ref[j] + got_ref[j])
        out_ref[j, :rows] = code
        out_ref[j, rows:] = head


def mirror_kernel(
    list_ref, count_ref, held_ref, own_ref, other_ref, tiles_ref, out_ref, msg, acc
):
    pieces, rows, classes = own_ref.shape[0], own_ref.shape[1] - HEAD, own_ref.shape[2]
    size = tiles_ref.shape[-1]
    row_tiles = msg.shape[0] // size
    col_tiles = acc.shape[0] // size - 1
    core = lax.rem(lax.axis_index("bcol"), 2)
    for j in range(pieces):
        for ref, column in ((own_ref, 2 * j + core), (other_ref, 2 * j + 1 - core)):
            high, low = split(decode(ref[j]))
            where = pl.ds(held_at(held_ref, column, rows), rows)
            msg[where, :classes] = high
            msg[where, classes:] = low
    acc[...] = jnp.zeros_like(acc)

    def body(s, carry):
        row, col, live, same = place(list_ref, count_ref, s, row_tiles, col_tiles)
        part = lax.dot_general(
            tiles_ref[s], msg[pl.ds(pl.multiple_of(row * size, size), size), :],
            (((0,), (0,)), ((), ())), preferred_element_type=jnp.float32,
        )
        col = jnp.where(live & jnp.logical_not(same), col, col_tiles)
        where = pl.ds(pl.multiple_of(col * size, size), size)
        acc[where, :] += part[:, :classes] + part[:, classes:]
        return carry

    lax.fori_loop(0, tiles_ref.shape[0], body, 0, unroll=16)
    for i in range(out_ref.shape[0]):
        code, head = encode(acc[i * rows : (i + 1) * rows, :])
        out_ref[i, :rows] = code
        out_ref[i, rows:] = head


def total_of(ref):
    total = decode(ref[0])
    for i in range(1, ref.shape[0]):
        total = total + decode(ref[i])
    return total


def sum_kernel(got_ref, out_ref):
    out_ref[...] = total_of(got_ref)


def next_field(got_ref, row_ref, scores_ref, scale_ref, seed_ref):
    total = total_of(got_ref) + row_ref[...]
    return jnp.where(seed_ref[...] > 0.0, scores_ref[...], total / scale_ref[...])


def middle_kernel(got_ref, row_ref, scores_ref, scale_ref, seed_ref, copies_ref, one_ref):
    field = next_field(got_ref, row_ref, scores_ref, scale_ref, seed_ref)
    put_message(field, copies_ref, one_ref)


def last_kernel(got_ref, row_ref, scores_ref, scale_ref, seed_ref, out_ref):
    out_ref[...] = next_field(got_ref, row_ref, scores_ref, scale_ref, seed_ref)


def hops(a, b):
    def chip(device):
        r, c = device
        return c // 8, r // 2, c // 2 % 4 * 2 + r % 2

    steps = (abs(i - j) for i, j in zip(chip(a), chip(b)))
    return sum(min(step, length - step) for step, length in zip(steps, (4, 8, 8)))


def cheapest(cost):
    n = len(cost)
    u, v, match, way = [0] * (n + 1), [0] * (n + 1), [0] * (n + 1), [0] * (n + 1)
    for i in range(1, n + 1):
        match[0], j0 = i, 0
        least, used = [math.inf] * (n + 1), [False] * (n + 1)
        while match[j0]:
            used[j0] = True
            i0, delta, j1 = match[j0], math.inf, 0
            for j in range(1, n + 1):
                if not used[j]:
                    now = cost[i0 - 1][j - 1] - u[i0] - v[j]
                    if now < least[j]:
                        least[j], way[j] = now, j0
                    if least[j] < delta:
                        delta, j1 = least[j], j
            for j in range(n + 1):
                if used[j]:
                    u[match[j]] += delta
                    v[j] -= delta
                else:
                    least[j] -= delta
            j0 = j1
        while j0:
            match[j0] = match[way[j0]]
            j0 = way[j0]
    columns = [0] * n
    for j in range(1, n + 1):
        columns[match[j] - 1] = j - 1
    return columns


def holders(n_brow, n_bcol):
    pairs, pieces = [], []
    for r in range(n_brow):
        owners = [(b, c) for c in range(r, n_bcol, n_brow) for b in range(n_brow)]
        cost = [[hops(owner, (r, k)) ** 6 for k in range(n_bcol)] for owner in owners]
        held = [0] * n_bcol
        for (b, c), k in zip(owners, cheapest(cost)):
            pairs.append((b * n_bcol + c, r * n_bcol + k))
            held[k] = 2 * (b // 2 * (n_bcol // n_brow) + c // n_brow) + b % 2
        pieces.append(held)
    return pairs, pieces


WHOLE = pl.BlockSpec(memory_space=pltpu.VMEM)
SCALARS = pl.BlockSpec(memory_space=pltpu.SMEM)
ANYWHERE = pl.BlockSpec(memory_space=pl.ANY)


def call(kernel, name, outs, args, specs=None, scratch=()):
    single = not isinstance(outs, (tuple, list))
    return pl.pallas_call(
        kernel,
        out_shape=outs,
        in_specs=specs or [WHOLE] * len(args),
        out_specs=WHOLE if single else tuple(WHOLE for _ in outs),
        scratch_shapes=list(scratch),
        compiler_params=pltpu.CompilerParams(vmem_limit_bytes=VMEM),
        name=name,
    )(*args)


def on_device(scores, degree, seed_mask, tiles, tile_list, tile_count):
    n_brow = lax.axis_size("brow")
    n_bcol = lax.axis_size("bcol")
    ratio = n_bcol // n_brow
    rows = scores.shape[1]
    classes = scores.shape[2]
    capacity = tiles.shape[2]
    size = tiles.shape[-1]
    col_tiles = n_brow * rows // size
    row_tiles = ratio * col_tiles
    stored = tiles[0, 0]
    slots = tile_list[0, 0]
    pairs, pieces = holders(n_brow, n_bcol)
    held = jnp.asarray(pieces, jnp.int32)
    initial = scores[0]
    seeds = jnp.broadcast_to(seed_mask[0].astype(jnp.float32)[:, None], (rows, classes))
    scale = jnp.broadcast_to(degree[0].astype(jnp.float32)[:, None], (rows, classes))

    half = n_bcol // 2
    groups = [[2 * j + k for j in range(half)] for k in range(2)]
    exchange = [(i, i ^ 1) for i in range(n_bcol)]
    back = [(holder, owner) for owner, holder in pairs]

    def swap(value, way):
        return lax.ppermute(value, ("brow", "bcol"), way)

    def over_brow(value):
        return lax.all_to_all(value, "brow", split_axis=0, concat_axis=0, tiled=True)

    def over_bcol(value):
        return lax.all_to_all(
            value, "bcol", split_axis=0, concat_axis=0, tiled=True, axis_index_groups=groups
        )

    piece = jax.ShapeDtypeStruct((rows + HEAD, classes), jnp.int16)
    brow_pieces = jax.ShapeDtypeStruct((n_brow,) + piece.shape, jnp.int16)
    bcol_pieces = jax.ShapeDtypeStruct((half,) + piece.shape, jnp.int16)
    sums = jax.ShapeDtypeStruct((half, rows, classes), jnp.float32)
    share = jax.ShapeDtypeStruct((rows, classes), jnp.float32)

    copies, one = call(first_kernel, "first", (brow_pieces, piece), (initial,))
    for sweep in range(SWEEPS):
        col_got = over_brow(copies)
        other = swap(one, pairs)
        before = col_got if sweep == 0 else other
        copies = call(copies_kernel, "copies", bcol_pieces, (before, other), [ANYWHERE, WHOLE])
        row_own = over_bcol(copies)
        keep, send = call(
            forward_kernel, "forward", (sums, sums), (slots, tile_count, held, col_got, stored),
            [SCALARS, SCALARS, SCALARS, WHOLE, WHOLE],
            [pltpu.VMEM((col_tiles * size, 2 * classes), jnp.bfloat16),
             pltpu.VMEM(((row_tiles + 1) * size, classes), jnp.float32)],
        )
        got = lax.ppermute(send, "bcol", exchange)
        joined = call(join_kernel, "join", bcol_pieces, (keep, got))
        row_got = over_bcol(joined)
        row_other = lax.ppermute(row_own, "bcol", exchange)
        col_parts = call(
            mirror_kernel, "mirror", brow_pieces,
            (slots, tile_count, held, row_own, row_other, stored),
            [SCALARS, SCALARS, SCALARS, WHOLE, WHOLE, WHOLE],
            [pltpu.VMEM((row_tiles * size, 2 * classes), jnp.bfloat16),
             pltpu.VMEM(((col_tiles + 1) * size, classes), jnp.float32)],
        )
        col_sums = over_brow(col_parts)
        row_sum = swap(call(sum_kernel, "sum", share, (row_got,)), back)
        args = (col_sums, row_sum, initial, scale, seeds)
        if sweep < SWEEPS - 1:
            copies, one = call(middle_kernel, "middle", (brow_pieces, piece), args)
        else:
            field = call(last_kernel, "last", share, args)
    return field[None]


def solution(mesh):
    placed = (
        P("bcol", "brow", None),
        P("bcol", "brow"),
        P("bcol", "brow"),
        P("brow", "bcol", None, None, None),
        P("brow", "bcol", None, None),
        P("brow", "bcol"),
    )
    return jax.shard_map(
        on_device, mesh=mesh, in_specs=placed, out_specs=P("bcol", "brow", None), check_vma=False
    )
```

```python
import math

import jax
import jax.numpy as jnp
from jax import lax
from jax.experimental import pallas as pl
from jax.experimental.pallas import tpu as pltpu
from jax.sharding import PartitionSpec as P

SWEEPS = 2
HEAD = 16
STEPS = 3840.0
SCALE_STEPS = 64.0
TINY = 1e-37
VMEM = 24 * 1024 * 1024


def encode(x):
    biggest = jnp.max(jnp.max(x, axis=0, keepdims=True), axis=1, keepdims=True)
    scale = jnp.floor(jnp.log(jnp.maximum(biggest, TINY)) * SCALE_STEPS) + 2.0
    below = jnp.log(jnp.maximum(x, TINY)) - scale * (1.0 / SCALE_STEPS)
    code = jnp.clip(below * STEPS + 65535.5, 0.0, 65535.0)
    code = jnp.where(x > 0.0, code, 0.0).astype(jnp.int32) - 32768
    head = jnp.broadcast_to(scale, (HEAD, x.shape[1])).astype(jnp.int32)
    return code.astype(jnp.int16), head.astype(jnp.int16)


def decode(piece):
    rows = piece.shape[0] - HEAD
    code = piece[:rows].astype(jnp.int32).astype(jnp.float32)
    head = piece[rows:].astype(jnp.int32).astype(jnp.float32)[:1]
    base = head * (1.0 / SCALE_STEPS) - 32767.0 / STEPS
    return jnp.where(code > -32768.0, jnp.exp(code * (1.0 / STEPS) + base), 0.0)


def weighted(field):
    total = jnp.maximum(jnp.sum(field, axis=-1, keepdims=True), TINY)
    share = field / total
    entropy = -jnp.sum(share * jnp.log(jnp.maximum(share, TINY)), axis=-1, keepdims=True)
    return (2.0 - entropy / math.log(field.shape[-1])) * field


def put_message(field, copies_ref, one_ref):
    rows = field.shape[0]
    code, head = encode(weighted(field))
    one_ref[:rows] = code
    one_ref[rows:] = head
    for i in range(copies_ref.shape[0]):
        copies_ref[i, :rows] = code
        copies_ref[i, rows:] = head


def split(value):
    high = value.astype(jnp.bfloat16)
    return high, (value - high.astype(jnp.float32)).astype(jnp.bfloat16)


def first_kernel(scores_ref, copies_ref, one_ref):
    put_message(scores_ref[...], copies_ref, one_ref)


def copies_kernel(after_ref, one_ref, copies_ref):
    for i in range(copies_ref.shape[0]):
        copies_ref[i] = one_ref[...]


def place(list_ref, count_ref, slot, row_tiles, col_tiles):
    n_brow, n_bcol = lax.axis_size("brow"), lax.axis_size("bcol")
    row = jnp.clip(list_ref[0, slot], 0, row_tiles - 1)
    col = jnp.clip(list_ref[1, slot], 0, col_tiles - 1)
    live = slot < count_ref[0, 0]
    same = lax.axis_index("brow") + n_brow * row == lax.axis_index("bcol") + n_bcol * col
    return row, col, live, same


def held_at(held_ref, column, rows):
    return pl.multiple_of(held_ref[lax.axis_index("brow"), column] * rows, rows)


def forward_kernel(
    list_ref, count_ref, held_ref, got_ref, tiles_ref, keep_ref, send_ref, msg, acc
):
    pieces, rows, classes = got_ref.shape[0], got_ref.shape[1] - HEAD, got_ref.shape[2]
    size = tiles_ref.shape[-1]
    col_tiles = msg.shape[0] // size
    row_tiles = acc.shape[0] // size - 1
    for i in range(pieces):
        high, low = split(decode(got_ref[i]))
        msg[i * rows : (i + 1) * rows, :classes] = high
        msg[i * rows : (i + 1) * rows, classes:] = low
    acc[...] = jnp.zeros_like(acc)

    def body(s, carry):
        row, col, live, _ = place(list_ref, count_ref, s, row_tiles, col_tiles)
        part = jnp.dot(
            tiles_ref[s], msg[pl.ds(pl.multiple_of(col * size, size), size), :],
            preferred_element_type=jnp.float32,
        )
        row = jnp.where(live, row, row_tiles)
        where = pl.ds(pl.multiple_of(row * size, size), size)
        acc[where, :] += part[:, :classes] + part[:, classes:]
        return carry

    lax.fori_loop(0, tiles_ref.shape[0], body, 0, unroll=64)
    core = lax.rem(lax.axis_index("bcol"), 2)
    for j in range(keep_ref.shape[0]):
        keep_ref[j] = acc[pl.ds(held_at(held_ref, 2 * j + core, rows), rows), :]
        send_ref[j] = acc[pl.ds(held_at(held_ref, 2 * j + 1 - core, rows), rows), :]


def join_kernel(keep_ref, got_ref, out_ref):
    rows = keep_ref.shape[1]
    for j in range(keep_ref.shape[0]):
        code, head = encode(keep_ref[j] + got_ref[j])
        out_ref[j, :rows] = code
        out_ref[j, rows:] = head


def mirror_kernel(
    list_ref, count_ref, held_ref, own_ref, other_ref, tiles_ref, out_ref, msg, acc
):
    pieces, rows, classes = own_ref.shape[0], own_ref.shape[1] - HEAD, own_ref.shape[2]
    size = tiles_ref.shape[-1]
    row_tiles = msg.shape[0] // size
    col_tiles = acc.shape[0] // size - 1
    core = lax.rem(lax.axis_index("bcol"), 2)
    for j in range(pieces):
        for ref, column in ((own_ref, 2 * j + core), (other_ref, 2 * j + 1 - core)):
            high, low = split(decode(ref[j]))
            where = pl.ds(held_at(held_ref, column, rows), rows)
            msg[where, :classes] = high
            msg[where, classes:] = low
    acc[...] = jnp.zeros_like(acc)

    def body(s, carry):
        row, col, live, same = place(list_ref, count_ref, s, row_tiles, col_tiles)
        part = lax.dot_general(
            tiles_ref[s], msg[pl.ds(pl.multiple_of(row * size, size), size), :],
            (((0,), (0,)), ((), ())), preferred_element_type=jnp.float32,
        )
        col = jnp.where(live & jnp.logical_not(same), col, col_tiles)
        where = pl.ds(pl.multiple_of(col * size, size), size)
        acc[where, :] += part[:, :classes] + part[:, classes:]
        return carry

    lax.fori_loop(0, tiles_ref.shape[0], body, 0, unroll=64)
    for i in range(out_ref.shape[0]):
        code, head = encode(acc[i * rows : (i + 1) * rows, :])
        out_ref[i, :rows] = code
        out_ref[i, rows:] = head


def total_of(ref):
    total = decode(ref[0])
    for i in range(1, ref.shape[0]):
        total = total + decode(ref[i])
    return total


def sum_kernel(got_ref, out_ref):
    out_ref[...] = total_of(got_ref)


def next_field(got_ref, row_ref, scores_ref, scale_ref, seed_ref):
    total = total_of(got_ref) + row_ref[...]
    return jnp.where(seed_ref[...] > 0.0, scores_ref[...], total / scale_ref[...])


def middle_kernel(got_ref, row_ref, scores_ref, scale_ref, seed_ref, copies_ref, one_ref):
    field = next_field(got_ref, row_ref, scores_ref, scale_ref, seed_ref)
    put_message(field, copies_ref, one_ref)


def last_kernel(got_ref, row_ref, scores_ref, scale_ref, seed_ref, out_ref):
    out_ref[...] = next_field(got_ref, row_ref, scores_ref, scale_ref, seed_ref)


def hops(a, b):
    def chip(device):
        r, c = device
        return c // 8, r // 2, c // 2 % 4 * 2 + r % 2

    steps = (abs(i - j) for i, j in zip(chip(a), chip(b)))
    return sum(min(step, length - step) for step, length in zip(steps, (4, 8, 8)))


def cheapest(cost):
    n = len(cost)
    u, v, match, way = [0] * (n + 1), [0] * (n + 1), [0] * (n + 1), [0] * (n + 1)
    for i in range(1, n + 1):
        match[0], j0 = i, 0
        least, used = [math.inf] * (n + 1), [False] * (n + 1)
        while match[j0]:
            used[j0] = True
            i0, delta, j1 = match[j0], math.inf, 0
            for j in range(1, n + 1):
                if not used[j]:
                    now = cost[i0 - 1][j - 1] - u[i0] - v[j]
                    if now < least[j]:
                        least[j], way[j] = now, j0
                    if least[j] < delta:
                        delta, j1 = least[j], j
            for j in range(n + 1):
                if used[j]:
                    u[match[j]] += delta
                    v[j] -= delta
                else:
                    least[j] -= delta
            j0 = j1
        while j0:
            match[j0] = match[way[j0]]
            j0 = way[j0]
    columns = [0] * n
    for j in range(1, n + 1):
        columns[match[j] - 1] = j - 1
    return columns


def holders(n_brow, n_bcol):
    pairs, pieces = [], []
    for r in range(n_brow):
        owners = [(b, c) for c in range(r, n_bcol, n_brow) for b in range(n_brow)]
        cost = [[hops(owner, (r, k)) ** 6 for k in range(n_bcol)] for owner in owners]
        held = [0] * n_bcol
        for (b, c), k in zip(owners, cheapest(cost)):
            pairs.append((b * n_bcol + c, r * n_bcol + k))
            held[k] = 2 * (b // 2 * (n_bcol // n_brow) + c // n_brow) + b % 2
        pieces.append(held)
    return pairs, pieces


WHOLE = pl.BlockSpec(memory_space=pltpu.VMEM)
SCALARS = pl.BlockSpec(memory_space=pltpu.SMEM)
ANYWHERE = pl.BlockSpec(memory_space=pl.ANY)


def call(kernel, name, outs, args, specs=None, scratch=()):
    single = not isinstance(outs, (tuple, list))
    return pl.pallas_call(
        kernel,
        out_shape=outs,
        in_specs=specs or [WHOLE] * len(args),
        out_specs=WHOLE if single else tuple(WHOLE for _ in outs),
        scratch_shapes=list(scratch),
        compiler_params=pltpu.CompilerParams(vmem_limit_bytes=VMEM),
        name=name,
    )(*args)


def on_device(scores, degree, seed_mask, tiles, tile_list, tile_count):
    n_brow = lax.axis_size("brow")
    n_bcol = lax.axis_size("bcol")
    ratio = n_bcol // n_brow
    rows = scores.shape[1]
    classes = scores.shape[2]
    capacity = tiles.shape[2]
    size = tiles.shape[-1]
    col_tiles = n_brow * rows // size
    row_tiles = ratio * col_tiles
    stored = tiles[0, 0]
    slots = tile_list[0, 0]
    pairs, pieces = holders(n_brow, n_bcol)
    held = jnp.asarray(pieces, jnp.int32)
    initial = scores[0]
    seeds = jnp.broadcast_to(seed_mask[0].astype(jnp.float32)[:, None], (rows, classes))
    scale = jnp.broadcast_to(degree[0].astype(jnp.float32)[:, None], (rows, classes))

    half = n_bcol // 2
    groups = [[2 * j + k for j in range(half)] for k in range(2)]
    exchange = [(i, i ^ 1) for i in range(n_bcol)]
    back = [(holder, owner) for owner, holder in pairs]

    def swap(value, way):
        return lax.ppermute(value, ("brow", "bcol"), way)

    def over_brow(value):
        return lax.all_to_all(value, "brow", split_axis=0, concat_axis=0, tiled=True)

    def over_bcol(value):
        return lax.all_to_all(
            value, "bcol", split_axis=0, concat_axis=0, tiled=True, axis_index_groups=groups
        )

    piece = jax.ShapeDtypeStruct((rows + HEAD, classes), jnp.int16)
    brow_pieces = jax.ShapeDtypeStruct((n_brow,) + piece.shape, jnp.int16)
    bcol_pieces = jax.ShapeDtypeStruct((half,) + piece.shape, jnp.int16)
    sums = jax.ShapeDtypeStruct((half, rows, classes), jnp.float32)
    share = jax.ShapeDtypeStruct((rows, classes), jnp.float32)

    copies, one = call(first_kernel, "first", (brow_pieces, piece), (initial,))
    for sweep in range(SWEEPS):
        col_got = over_brow(copies)
        other = swap(one, pairs)
        before = col_got if sweep == 0 else other
        copies = call(copies_kernel, "copies", bcol_pieces, (before, other), [ANYWHERE, WHOLE])
        row_own = over_bcol(copies)
        keep, send = call(
            forward_kernel, "forward", (sums, sums), (slots, tile_count, held, col_got, stored),
            [SCALARS, SCALARS, SCALARS, WHOLE, WHOLE],
            [pltpu.VMEM((col_tiles * size, 2 * classes), jnp.bfloat16),
             pltpu.VMEM(((row_tiles + 1) * size, classes), jnp.float32)],
        )
        got = lax.ppermute(send, "bcol", exchange)
        joined = call(join_kernel, "join", bcol_pieces, (keep, got))
        row_got = over_bcol(joined)
        row_other = lax.ppermute(row_own, "bcol", exchange)
        col_parts = call(
            mirror_kernel, "mirror", brow_pieces,
            (slots, tile_count, held, row_own, row_other, stored),
            [SCALARS, SCALARS, SCALARS, WHOLE, WHOLE, WHOLE],
            [pltpu.VMEM((row_tiles * size, 2 * classes), jnp.bfloat16),
             pltpu.VMEM(((col_tiles + 1) * size, classes), jnp.float32)],
        )
        col_sums = over_brow(col_parts)
        row_sum = swap(call(sum_kernel, "sum", share, (row_got,)), back)
        args = (col_sums, row_sum, initial, scale, seeds)
        if sweep < SWEEPS - 1:
            copies, one = call(middle_kernel, "middle", (brow_pieces, piece), args)
        else:
            field = call(last_kernel, "last", share, args)
    return field[None]


def solution(mesh):
    placed = (
        P("bcol", "brow", None),
        P("bcol", "brow"),
        P("bcol", "brow"),
        P("brow", "bcol", None, None, None),
        P("brow", "bcol", None, None),
        P("brow", "bcol"),
    )
    return jax.shard_map(
        on_device, mesh=mesh, in_specs=placed, out_specs=P("bcol", "brow", None), check_vma=False
    )
```

```python
import math

import jax
import jax.numpy as jnp
from jax import lax
from jax.experimental import pallas as pl
from jax.experimental.pallas import tpu as pltpu
from jax.sharding import PartitionSpec as P

SWEEPS = 2
HEAD = 16
STEPS = 3840.0
SCALE_STEPS = 64.0
TINY = 1e-37
VMEM = 24 * 1024 * 1024


def encode(x):
    biggest = jnp.max(jnp.max(x, axis=0, keepdims=True), axis=1, keepdims=True)
    scale = jnp.floor(jnp.log(jnp.maximum(biggest, TINY)) * SCALE_STEPS) + 2.0
    below = jnp.log(jnp.maximum(x, TINY)) - scale * (1.0 / SCALE_STEPS)
    code = jnp.clip(below * STEPS + 65535.5, 0.0, 65535.0)
    code = jnp.where(x > 0.0, code, 0.0).astype(jnp.int32) - 32768
    head = jnp.broadcast_to(scale, (HEAD, x.shape[1])).astype(jnp.int32)
    return code.astype(jnp.int16), head.astype(jnp.int16)


def decode(piece):
    rows = piece.shape[0] - HEAD
    code = piece[:rows].astype(jnp.int32).astype(jnp.float32)
    head = piece[rows:].astype(jnp.int32).astype(jnp.float32)[:1]
    base = head * (1.0 / SCALE_STEPS) - 32767.0 / STEPS
    return jnp.where(code > -32768.0, jnp.exp(code * (1.0 / STEPS) + base), 0.0)


def weighted(field):
    total = jnp.maximum(jnp.sum(field, axis=-1, keepdims=True), TINY)
    share = field / total
    entropy = -jnp.sum(share * jnp.log(jnp.maximum(share, TINY)), axis=-1, keepdims=True)
    return (2.0 - entropy / math.log(field.shape[-1])) * field


def put_message(field, copies_ref, one_ref):
    rows = field.shape[0]
    code, head = encode(weighted(field))
    one_ref[:rows] = code
    one_ref[rows:] = head
    for i in range(copies_ref.shape[0]):
        copies_ref[i, :rows] = code
        copies_ref[i, rows:] = head


def split(value):
    high = value.astype(jnp.bfloat16)
    return high, (value - high.astype(jnp.float32)).astype(jnp.bfloat16)


def first_kernel(tiles_ref, slots_ref, scores_ref, copies_ref, one_ref):
    put_message(scores_ref[...], copies_ref, one_ref)


def copies_kernel(after_ref, one_ref, copies_ref):
    for i in range(copies_ref.shape[0]):
        copies_ref[i] = one_ref[...]


def place(list_ref, count_ref, slot, row_tiles, col_tiles):
    n_brow, n_bcol = lax.axis_size("brow"), lax.axis_size("bcol")
    row = jnp.clip(list_ref[0, slot], 0, row_tiles - 1)
    col = jnp.clip(list_ref[1, slot], 0, col_tiles - 1)
    live = slot < count_ref[0, 0]
    same = lax.axis_index("brow") + n_brow * row == lax.axis_index("bcol") + n_bcol * col
    return row, col, live, same


def held_at(held_ref, column, rows):
    return pl.multiple_of(held_ref[lax.axis_index("brow"), column] * rows, rows)


def forward_kernel(
    list_ref, count_ref, held_ref, got_ref, tiles_ref, keep_ref, send_ref, msg, acc
):
    pieces, rows, classes = got_ref.shape[0], got_ref.shape[1] - HEAD, got_ref.shape[2]
    size = tiles_ref.shape[-1]
    col_tiles = msg.shape[0] // size
    row_tiles = acc.shape[0] // size - 1
    for i in range(pieces):
        high, low = split(decode(got_ref[i]))
        msg[i * rows : (i + 1) * rows, :classes] = high
        msg[i * rows : (i + 1) * rows, classes:] = low
    acc[...] = jnp.zeros_like(acc)

    def body(s, carry):
        row, col, live, _ = place(list_ref, count_ref, s, row_tiles, col_tiles)
        part = jnp.dot(
            tiles_ref[s], msg[pl.ds(pl.multiple_of(col * size, size), size), :],
            preferred_element_type=jnp.float32,
        )
        row = jnp.where(live, row, row_tiles)
        where = pl.ds(pl.multiple_of(row * size, size), size)
        acc[where, :] += part[:, :classes] + part[:, classes:]
        return carry

    lax.fori_loop(0, tiles_ref.shape[0], body, 0, unroll=64)
    core = lax.rem(lax.axis_index("bcol"), 2)
    for j in range(keep_ref.shape[0]):
        keep_ref[j] = acc[pl.ds(held_at(held_ref, 2 * j + core, rows), rows), :]
        send_ref[j] = acc[pl.ds(held_at(held_ref, 2 * j + 1 - core, rows), rows), :]


def join_kernel(keep_ref, got_ref, out_ref):
    rows = keep_ref.shape[1]
    for j in range(keep_ref.shape[0]):
        code, head = encode(keep_ref[j] + got_ref[j])
        out_ref[j, :rows] = code
        out_ref[j, rows:] = head


def mirror_kernel(
    list_ref, count_ref, held_ref, own_ref, other_ref, tiles_ref, out_ref, msg, acc
):
    pieces, rows, classes = own_ref.shape[0], own_ref.shape[1] - HEAD, own_ref.shape[2]
    size = tiles_ref.shape[-1]
    row_tiles = msg.shape[0] // size
    col_tiles = acc.shape[0] // size - 1
    core = lax.rem(lax.axis_index("bcol"), 2)
    for j in range(pieces):
        for ref, column in ((own_ref, 2 * j + core), (other_ref, 2 * j + 1 - core)):
            high, low = split(decode(ref[j]))
            where = pl.ds(held_at(held_ref, column, rows), rows)
            msg[where, :classes] = high
            msg[where, classes:] = low
    acc[...] = jnp.zeros_like(acc)

    def body(s, carry):
        row, col, live, same = place(list_ref, count_ref, s, row_tiles, col_tiles)
        part = lax.dot_general(
            tiles_ref[s], msg[pl.ds(pl.multiple_of(row * size, size), size), :],
            (((0,), (0,)), ((), ())), preferred_element_type=jnp.float32,
        )
        col = jnp.where(live & jnp.logical_not(same), col, col_tiles)
        where = pl.ds(pl.multiple_of(col * size, size), size)
        acc[where, :] += part[:, :classes] + part[:, classes:]
        return carry

    lax.fori_loop(0, tiles_ref.shape[0], body, 0, unroll=64)
    for i in range(out_ref.shape[0]):
        code, head = encode(acc[i * rows : (i + 1) * rows, :])
        out_ref[i, :rows] = code
        out_ref[i, rows:] = head


def total_of(ref):
    total = decode(ref[0])
    for i in range(1, ref.shape[0]):
        total = total + decode(ref[i])
    return total


def sum_kernel(got_ref, out_ref):
    out_ref[...] = total_of(got_ref)


def next_field(got_ref, row_ref, scores_ref, scale_ref, seed_ref):
    total = total_of(got_ref) + row_ref[...]
    return jnp.where(seed_ref[...] > 0.0, scores_ref[...], total / scale_ref[...])


def middle_kernel(got_ref, row_ref, scores_ref, scale_ref, seed_ref, copies_ref, one_ref):
    field = next_field(got_ref, row_ref, scores_ref, scale_ref, seed_ref)
    put_message(field, copies_ref, one_ref)


def last_kernel(got_ref, row_ref, scores_ref, scale_ref, seed_ref, out_ref):
    out_ref[...] = next_field(got_ref, row_ref, scores_ref, scale_ref, seed_ref)


def hops(a, b):
    def chip(device):
        r, c = device
        return c // 8, r // 2, c // 2 % 4 * 2 + r % 2

    steps = (abs(i - j) for i, j in zip(chip(a), chip(b)))
    return sum(min(step, length - step) for step, length in zip(steps, (4, 8, 8)))


def cheapest(cost):
    n = len(cost)
    u, v, match, way = [0] * (n + 1), [0] * (n + 1), [0] * (n + 1), [0] * (n + 1)
    for i in range(1, n + 1):
        match[0], j0 = i, 0
        least, used = [math.inf] * (n + 1), [False] * (n + 1)
        while match[j0]:
            used[j0] = True
            i0, delta, j1 = match[j0], math.inf, 0
            for j in range(1, n + 1):
                if not used[j]:
                    now = cost[i0 - 1][j - 1] - u[i0] - v[j]
                    if now < least[j]:
                        least[j], way[j] = now, j0
                    if least[j] < delta:
                        delta, j1 = least[j], j
            for j in range(n + 1):
                if used[j]:
                    u[match[j]] += delta
                    v[j] -= delta
                else:
                    least[j] -= delta
            j0 = j1
        while j0:
            match[j0] = match[way[j0]]
            j0 = way[j0]
    columns = [0] * n
    for j in range(1, n + 1):
        columns[match[j] - 1] = j - 1
    return columns


def holders(n_brow, n_bcol):
    pairs, pieces = [], []
    for r in range(n_brow):
        owners = [(b, c) for c in range(r, n_bcol, n_brow) for b in range(n_brow)]
        cost = [[hops(owner, (r, k)) ** 6 for k in range(n_bcol)] for owner in owners]
        held = [0] * n_bcol
        for (b, c), k in zip(owners, cheapest(cost)):
            pairs.append((b * n_bcol + c, r * n_bcol + k))
            held[k] = 2 * (b // 2 * (n_bcol // n_brow) + c // n_brow) + b % 2
        pieces.append(held)
    return pairs, pieces


WHOLE = pl.BlockSpec(memory_space=pltpu.VMEM)
SCALARS = pl.BlockSpec(memory_space=pltpu.SMEM)
ANYWHERE = pl.BlockSpec(memory_space=pl.ANY)


def call(kernel, name, outs, args, specs=None, scratch=()):
    single = not isinstance(outs, (tuple, list))
    return pl.pallas_call(
        kernel,
        out_shape=outs,
        in_specs=specs or [WHOLE] * len(args),
        out_specs=WHOLE if single else tuple(WHOLE for _ in outs),
        scratch_shapes=list(scratch),
        compiler_params=pltpu.CompilerParams(vmem_limit_bytes=VMEM),
        name=name,
    )(*args)


def on_device(scores, degree, seed_mask, tiles, tile_list, tile_count):
    n_brow = lax.axis_size("brow")
    n_bcol = lax.axis_size("bcol")
    ratio = n_bcol // n_brow
    rows = scores.shape[1]
    classes = scores.shape[2]
    capacity = tiles.shape[2]
    size = tiles.shape[-1]
    col_tiles = n_brow * rows // size
    row_tiles = ratio * col_tiles
    stored = tiles[0, 0]
    slots = tile_list[0, 0]
    pairs, pieces = holders(n_brow, n_bcol)
    held = jnp.asarray(pieces, jnp.int32)
    initial = scores[0]
    seeds = jnp.broadcast_to(seed_mask[0].astype(jnp.float32)[:, None], (rows, classes))
    scale = jnp.broadcast_to(degree[0].astype(jnp.float32)[:, None], (rows, classes))

    half = n_bcol // 2
    groups = [[2 * j + k for j in range(half)] for k in range(2)]
    exchange = [(i, i ^ 1) for i in range(n_bcol)]
    back = [(holder, owner) for owner, holder in pairs]

    def swap(value, way):
        return lax.ppermute(value, ("brow", "bcol"), way)

    def over_brow(value):
        return lax.all_to_all(value, "brow", split_axis=0, concat_axis=0, tiled=True)

    def over_bcol(value):
        return lax.all_to_all(
            value, "bcol", split_axis=0, concat_axis=0, tiled=True, axis_index_groups=groups
        )

    piece = jax.ShapeDtypeStruct((rows + HEAD, classes), jnp.int16)
    brow_pieces = jax.ShapeDtypeStruct((n_brow,) + piece.shape, jnp.int16)
    bcol_pieces = jax.ShapeDtypeStruct((half,) + piece.shape, jnp.int16)
    sums = jax.ShapeDtypeStruct((half, rows, classes), jnp.float32)
    share = jax.ShapeDtypeStruct((rows, classes), jnp.float32)

    copies, one = call(first_kernel, "first", (brow_pieces, piece), (stored, slots, initial),
                       [ANYWHERE, ANYWHERE, WHOLE])
    for sweep in range(SWEEPS):
        col_got = over_brow(copies)
        other = swap(one, pairs)
        before = col_got if sweep == 0 else other
        copies = call(copies_kernel, "copies", bcol_pieces, (before, other), [ANYWHERE, WHOLE])
        row_own = over_bcol(copies)
        keep, send = call(
            forward_kernel, "forward", (sums, sums), (slots, tile_count, held, col_got, stored),
            [SCALARS, SCALARS, SCALARS, WHOLE, WHOLE],
            [pltpu.VMEM((col_tiles * size, 2 * classes), jnp.bfloat16),
             pltpu.VMEM(((row_tiles + 1) * size, classes), jnp.float32)],
        )
        got = lax.ppermute(send, "bcol", exchange)
        joined = call(join_kernel, "join", bcol_pieces, (keep, got))
        row_got = over_bcol(joined)
        row_other = lax.ppermute(row_own, "bcol", exchange)
        col_parts = call(
            mirror_kernel, "mirror", brow_pieces,
            (slots, tile_count, held, row_own, row_other, stored),
            [SCALARS, SCALARS, SCALARS, WHOLE, WHOLE, WHOLE],
            [pltpu.VMEM((row_tiles * size, 2 * classes), jnp.bfloat16),
             pltpu.VMEM(((col_tiles + 1) * size, classes), jnp.float32)],
        )
        col_sums = over_brow(col_parts)
        row_sum = swap(call(sum_kernel, "sum", share, (row_got,)), back)
        args = (col_sums, row_sum, initial, scale, seeds)
        if sweep < SWEEPS - 1:
            copies, one = call(middle_kernel, "middle", (brow_pieces, piece), args)
        else:
            field = call(last_kernel, "last", share, args)
    return field[None]


def solution(mesh):
    placed = (
        P("bcol", "brow", None),
        P("bcol", "brow"),
        P("bcol", "brow"),
        P("brow", "bcol", None, None, None),
        P("brow", "bcol", None, None),
        P("brow", "bcol"),
    )
    return jax.shard_map(
        on_device, mesh=mesh, in_specs=placed, out_specs=P("bcol", "brow", None), check_vma=False
    )
```

```python
import math

import jax
import jax.numpy as jnp
from jax import lax
from jax.experimental import pallas as pl
from jax.experimental.pallas import tpu as pltpu
from jax.sharding import PartitionSpec as P

SWEEPS = 2
HEAD = 16
STEPS = 3840.0
SCALE_STEPS = 64.0
TINY = 1e-37
VMEM = 24 * 1024 * 1024


def encode(x):
    biggest = jnp.max(jnp.max(x, axis=0, keepdims=True), axis=1, keepdims=True)
    scale = jnp.floor(jnp.log(jnp.maximum(biggest, TINY)) * SCALE_STEPS) + 2.0
    below = jnp.log(jnp.maximum(x, TINY)) - scale * (1.0 / SCALE_STEPS)
    code = jnp.clip(below * STEPS + 65535.5, 0.0, 65535.0)
    code = jnp.where(x > 0.0, code, 0.0).astype(jnp.int32) - 32768
    head = jnp.broadcast_to(scale, (HEAD, x.shape[1])).astype(jnp.int32)
    return code.astype(jnp.int16), head.astype(jnp.int16)


def decode(piece):
    rows = piece.shape[0] - HEAD
    code = piece[:rows].astype(jnp.int32).astype(jnp.float32)
    head = piece[rows:].astype(jnp.int32).astype(jnp.float32)[:1]
    base = head * (1.0 / SCALE_STEPS) - 32767.0 / STEPS
    return jnp.where(code > -32768.0, jnp.exp(code * (1.0 / STEPS) + base), 0.0)


def weighted(field):
    total = jnp.maximum(jnp.sum(field, axis=-1, keepdims=True), TINY)
    share = field / total
    entropy = -jnp.sum(share * jnp.log(jnp.maximum(share, TINY)), axis=-1, keepdims=True)
    return (2.0 - entropy / math.log(field.shape[-1])) * field


def put_message(field, copies_ref, one_ref):
    rows = field.shape[0]
    code, head = encode(weighted(field))
    one_ref[:rows] = code
    one_ref[rows:] = head
    for i in range(copies_ref.shape[0]):
        copies_ref[i, :rows] = code
        copies_ref[i, rows:] = head


def split(value):
    high = value.astype(jnp.bfloat16)
    return high, (value - high.astype(jnp.float32)).astype(jnp.bfloat16)


def first_kernel(tiles_ref, slots_ref, count_ref, scores_ref, copies_ref, one_ref):
    put_message(scores_ref[...], copies_ref, one_ref)


def copies_kernel(after_ref, one_ref, copies_ref):
    for i in range(copies_ref.shape[0]):
        copies_ref[i] = one_ref[...]


def place(list_ref, count_ref, slot, row_tiles, col_tiles):
    n_brow, n_bcol = lax.axis_size("brow"), lax.axis_size("bcol")
    row = jnp.clip(list_ref[0, slot], 0, row_tiles - 1)
    col = jnp.clip(list_ref[1, slot], 0, col_tiles - 1)
    live = slot < count_ref[0, 0]
    same = lax.axis_index("brow") + n_brow * row == lax.axis_index("bcol") + n_bcol * col
    return row, col, live, same


def held_at(held_ref, column, rows):
    return pl.multiple_of(held_ref[lax.axis_index("brow"), column] * rows, rows)


def forward_kernel(
    list_ref, count_ref, held_ref, got_ref, tiles_ref, keep_ref, send_ref, msg, acc
):
    pieces, rows, classes = got_ref.shape[0], got_ref.shape[1] - HEAD, got_ref.shape[2]
    size = tiles_ref.shape[-1]
    col_tiles = msg.shape[0] // size
    row_tiles = acc.shape[0] // size - 1
    for i in range(pieces):
        high, low = split(decode(got_ref[i]))
        msg[i * rows : (i + 1) * rows, :classes] = high
        msg[i * rows : (i + 1) * rows, classes:] = low
    acc[...] = jnp.zeros_like(acc)

    def body(s, carry):
        row, col, live, _ = place(list_ref, count_ref, s, row_tiles, col_tiles)
        part = jnp.dot(
            tiles_ref[s], msg[pl.ds(pl.multiple_of(col * size, size), size), :],
            preferred_element_type=jnp.float32,
        )
        row = jnp.where(live, row, row_tiles)
        where = pl.ds(pl.multiple_of(row * size, size), size)
        acc[where, :] += part[:, :classes] + part[:, classes:]
        return carry

    lax.fori_loop(0, tiles_ref.shape[0], body, 0, unroll=64)
    core = lax.rem(lax.axis_index("bcol"), 2)
    for j in range(keep_ref.shape[0]):
        keep_ref[j] = acc[pl.ds(held_at(held_ref, 2 * j + core, rows), rows), :]
        send_ref[j] = acc[pl.ds(held_at(held_ref, 2 * j + 1 - core, rows), rows), :]


def join_kernel(keep_ref, got_ref, out_ref):
    rows = keep_ref.shape[1]
    for j in range(keep_ref.shape[0]):
        code, head = encode(keep_ref[j] + got_ref[j])
        out_ref[j, :rows] = code
        out_ref[j, rows:] = head


def mirror_kernel(
    list_ref, count_ref, held_ref, own_ref, other_ref, tiles_ref, out_ref, msg, acc
):
    pieces, rows, classes = own_ref.shape[0], own_ref.shape[1] - HEAD, own_ref.shape[2]
    size = tiles_ref.shape[-1]
    row_tiles = msg.shape[0] // size
    col_tiles = acc.shape[0] // size - 1
    core = lax.rem(lax.axis_index("bcol"), 2)
    for j in range(pieces):
        for ref, column in ((own_ref, 2 * j + core), (other_ref, 2 * j + 1 - core)):
            high, low = split(decode(ref[j]))
            where = pl.ds(held_at(held_ref, column, rows), rows)
            msg[where, :classes] = high
            msg[where, classes:] = low
    acc[...] = jnp.zeros_like(acc)

    def body(s, carry):
        row, col, live, same = place(list_ref, count_ref, s, row_tiles, col_tiles)
        part = lax.dot_general(
            tiles_ref[s], msg[pl.ds(pl.multiple_of(row * size, size), size), :],
            (((0,), (0,)), ((), ())), preferred_element_type=jnp.float32,
        )
        col = jnp.where(live & jnp.logical_not(same), col, col_tiles)
        where = pl.ds(pl.multiple_of(col * size, size), size)
        acc[where, :] += part[:, :classes] + part[:, classes:]
        return carry

    lax.fori_loop(0, tiles_ref.shape[0], body, 0, unroll=64)
    for i in range(out_ref.shape[0]):
        code, head = encode(acc[i * rows : (i + 1) * rows, :])
        out_ref[i, :rows] = code
        out_ref[i, rows:] = head


def total_of(ref):
    total = decode(ref[0])
    for i in range(1, ref.shape[0]):
        total = total + decode(ref[i])
    return total


def sum_kernel(got_ref, out_ref):
    out_ref[...] = total_of(got_ref)


def next_field(got_ref, row_ref, scores_ref, scale_ref, seed_ref):
    total = total_of(got_ref) + row_ref[...]
    return jnp.where(seed_ref[...] > 0.0, scores_ref[...], total / scale_ref[...])


def middle_kernel(got_ref, row_ref, scores_ref, scale_ref, seed_ref, copies_ref, one_ref):
    field = next_field(got_ref, row_ref, scores_ref, scale_ref, seed_ref)
    put_message(field, copies_ref, one_ref)


def last_kernel(got_ref, row_ref, scores_ref, scale_ref, seed_ref, out_ref):
    out_ref[...] = next_field(got_ref, row_ref, scores_ref, scale_ref, seed_ref)


def hops(a, b):
    def chip(device):
        r, c = device
        return c // 8, r // 2, c // 2 % 4 * 2 + r % 2

    steps = (abs(i - j) for i, j in zip(chip(a), chip(b)))
    return sum(min(step, length - step) for step, length in zip(steps, (4, 8, 8)))


def cheapest(cost):
    n = len(cost)
    u, v, match, way = [0] * (n + 1), [0] * (n + 1), [0] * (n + 1), [0] * (n + 1)
    for i in range(1, n + 1):
        match[0], j0 = i, 0
        least, used = [math.inf] * (n + 1), [False] * (n + 1)
        while match[j0]:
            used[j0] = True
            i0, delta, j1 = match[j0], math.inf, 0
            for j in range(1, n + 1):
                if not used[j]:
                    now = cost[i0 - 1][j - 1] - u[i0] - v[j]
                    if now < least[j]:
                        least[j], way[j] = now, j0
                    if least[j] < delta:
                        delta, j1 = least[j], j
            for j in range(n + 1):
                if used[j]:
                    u[match[j]] += delta
                    v[j] -= delta
                else:
                    least[j] -= delta
            j0 = j1
        while j0:
            match[j0] = match[way[j0]]
            j0 = way[j0]
    columns = [0] * n
    for j in range(1, n + 1):
        columns[match[j] - 1] = j - 1
    return columns


def holders(n_brow, n_bcol):
    pairs, pieces = [], []
    for r in range(n_brow):
        owners = [(b, c) for c in range(r, n_bcol, n_brow) for b in range(n_brow)]
        cost = [[hops(owner, (r, k)) ** 6 for k in range(n_bcol)] for owner in owners]
        held = [0] * n_bcol
        for (b, c), k in zip(owners, cheapest(cost)):
            pairs.append((b * n_bcol + c, r * n_bcol + k))
            held[k] = 2 * (b // 2 * (n_bcol // n_brow) + c // n_brow) + b % 2
        pieces.append(held)
    return pairs, pieces


WHOLE = pl.BlockSpec(memory_space=pltpu.VMEM)
SCALARS = pl.BlockSpec(memory_space=pltpu.SMEM)
ANYWHERE = pl.BlockSpec(memory_space=pl.ANY)


def call(kernel, name, outs, args, specs=None, scratch=()):
    single = not isinstance(outs, (tuple, list))
    return pl.pallas_call(
        kernel,
        out_shape=outs,
        in_specs=specs or [WHOLE] * len(args),
        out_specs=WHOLE if single else tuple(WHOLE for _ in outs),
        scratch_shapes=list(scratch),
        compiler_params=pltpu.CompilerParams(vmem_limit_bytes=VMEM),
        name=name,
    )(*args)


def on_device(scores, degree, seed_mask, tiles, tile_list, tile_count):
    n_brow = lax.axis_size("brow")
    n_bcol = lax.axis_size("bcol")
    ratio = n_bcol // n_brow
    rows = scores.shape[1]
    classes = scores.shape[2]
    capacity = tiles.shape[2]
    size = tiles.shape[-1]
    col_tiles = n_brow * rows // size
    row_tiles = ratio * col_tiles
    stored = tiles[0, 0]
    slots = tile_list[0, 0]
    pairs, pieces = holders(n_brow, n_bcol)
    held = jnp.asarray(pieces, jnp.int32)
    initial = scores[0]
    seeds = jnp.broadcast_to(seed_mask[0].astype(jnp.float32)[:, None], (rows, classes))
    scale = jnp.broadcast_to(degree[0].astype(jnp.float32)[:, None], (rows, classes))

    half = n_bcol // 2
    groups = [[2 * j + k for j in range(half)] for k in range(2)]
    exchange = [(i, i ^ 1) for i in range(n_bcol)]
    back = [(holder, owner) for owner, holder in pairs]

    def swap(value, way):
        return lax.ppermute(value, ("brow", "bcol"), way)

    def over_brow(value):
        return lax.all_to_all(value, "brow", split_axis=0, concat_axis=0, tiled=True)

    def over_bcol(value):
        return lax.all_to_all(
            value, "bcol", split_axis=0, concat_axis=0, tiled=True, axis_index_groups=groups
        )

    piece = jax.ShapeDtypeStruct((rows + HEAD, classes), jnp.int16)
    brow_pieces = jax.ShapeDtypeStruct((n_brow,) + piece.shape, jnp.int16)
    bcol_pieces = jax.ShapeDtypeStruct((half,) + piece.shape, jnp.int16)
    sums = jax.ShapeDtypeStruct((half, rows, classes), jnp.float32)
    share = jax.ShapeDtypeStruct((rows, classes), jnp.float32)

    copies, one = call(first_kernel, "first", (brow_pieces, piece), (stored, slots, tile_count, initial),
                       [ANYWHERE, ANYWHERE, SCALARS, WHOLE])
    for sweep in range(SWEEPS):
        col_got = over_brow(copies)
        other = swap(one, pairs)
        before = col_got if sweep == 0 else other
        copies = call(copies_kernel, "copies", bcol_pieces, (before, other), [ANYWHERE, WHOLE])
        row_own = over_bcol(copies)
        keep, send = call(
            forward_kernel, "forward", (sums, sums), (slots, tile_count, held, col_got, stored),
            [SCALARS, SCALARS, SCALARS, WHOLE, WHOLE],
            [pltpu.VMEM((col_tiles * size, 2 * classes), jnp.bfloat16),
             pltpu.VMEM(((row_tiles + 1) * size, classes), jnp.float32)],
        )
        got = lax.ppermute(send, "bcol", exchange)
        joined = call(join_kernel, "join", bcol_pieces, (keep, got))
        row_got = over_bcol(joined)
        row_other = lax.ppermute(row_own, "bcol", exchange)
        col_parts = call(
            mirror_kernel, "mirror", brow_pieces,
            (slots, tile_count, held, row_own, row_other, stored),
            [SCALARS, SCALARS, SCALARS, WHOLE, WHOLE, WHOLE],
            [pltpu.VMEM((row_tiles * size, 2 * classes), jnp.bfloat16),
             pltpu.VMEM(((col_tiles + 1) * size, classes), jnp.float32)],
        )
        col_sums = over_brow(col_parts)
        row_sum = swap(call(sum_kernel, "sum", share, (row_got,)), back)
        args = (col_sums, row_sum, initial, scale, seeds)
        if sweep < SWEEPS - 1:
            copies, one = call(middle_kernel, "middle", (brow_pieces, piece), args)
        else:
            field = call(last_kernel, "last", share, args)
    return field[None]


def solution(mesh):
    placed = (
        P("bcol", "brow", None),
        P("bcol", "brow"),
        P("bcol", "brow"),
        P("brow", "bcol", None, None, None),
        P("brow", "bcol", None, None),
        P("brow", "bcol"),
    )
    return jax.shard_map(
        on_device, mesh=mesh, in_specs=placed, out_specs=P("bcol", "brow", None), check_vma=False
    )
```
